32 devices in a mesh: outer: 8 (over y, x, core), inner: 4 (over z).
Axes of the slice: x: 2, y: 2, z: 4, core: 2. Of those that a mesh axis runs over, the one named last changes fastest.
Arguments:
- queries: bfloat16 [4096, 2048], P(('outer', 'inner')), may hold values from -6 to 6
- keys: bfloat16 [4096, 2048], P(('outer', 'inner')), may hold values from -6 to 6
- values: bfloat16 [4096, 2048], P(('outer', 'inner')), may hold values from -7 to 7
- cotangent: bfloat16 [4096, 2048], P(('outer', 'inner')), may hold values from -7 to 7
Outputs:
- attended: bfloat16 [4096, 2048], P(('outer', 'inner'))
- query_grad: bfloat16 [4096, 2048], P(('outer', 'inner'))
- key_grad: bfloat16 [4096, 2048], P(('outer', 'inner'))
- value_grad: bfloat16 [4096, 2048], P(('outer', 'inner'))
The draws below stay inside these ranges and needn't reach their ends.
All inputs are finite; a program needn't handle non-finite values.
Results may differ from the reference program's by a relative error of at most 0.013.
The reference program's roundings to bfloat16 on the way (of `q_feat`, `k_feat`, `weights`, `state_low`, `grad_scaled`, `grad_scores` and `later_low`) count: a program that leaves them out, or rounds other values in their place, can miss the bound.
Values sent between devices are 32-bit elements; how exact they have to be, the bound alone decides.
No kernel may reach another device: no remote copies, remote signals or barrier semaphores. Data moves between devices by JAX's collectives and lax.ppermute only.
A program may use at most 128 MiB of HBM per device.

```python
import jax
import jax.numpy as jnp
from jax import lax

HEADS = 16
HD = 128
TOK_DEV = 128
TOKENS = 4096


def shifted_normal(key, salt):
    key = jax.random.fold_in(key, salt)
    first, second = jax.random.split(key)
    blocks = TOKENS // TOK_DEV
    offset = jnp.clip(jax.random.normal(first, (blocks, 1, HEADS * HD), jnp.float32), -3.0, 3.0)
    noise = jnp.clip(jax.random.normal(second, (blocks, TOK_DEV, HEADS * HD), jnp.float32), -4.0, 4.0)
    return (offset + noise).reshape(TOKENS, HEADS * HD)


def draw_values(key, part):
    return shifted_normal(key, 11).astype(jnp.bfloat16)


def draw_cotangent(key, part):
    return shifted_normal(key, 23).astype(jnp.bfloat16)


def shard_levels(key, dims, cuts, smallest, largest):
    gain, own = 1.0, jax.random.fold_in(key, 6)
    for dim, blocks in cuts:
        draws = jnp.exp(jax.random.uniform(jax.random.fold_in(own, dim), (blocks,), jnp.float32, smallest / len(cuts), largest / len(cuts)))
        gain = gain * jnp.repeat(draws, dims[dim] // blocks).reshape([-1 if axis == dim else 1 for axis in range(len(dims))])
    return gain


def gaussian(stream_key, dims, scale, limit, cuts=(), kind=jnp.bfloat16):
    level = shard_levels(stream_key, dims, cuts, -0.22, 0.18) if cuts else 1.0
    entries = jax.random.normal(stream_key, dims, jnp.float32) * scale * level
    return jnp.minimum(jnp.maximum(entries, -limit), limit).astype(kind)


def setup_inputs(seed: int = 0) -> dict:
    key_of = jax.random.split(jax.random.key(seed), 5)
    queries = gaussian(key_of[0], (TOKENS, HEADS * HD), 1.0, 6.0, ((0, 32),))
    keys = gaussian(key_of[1], (TOKENS, HEADS * HD), 1.0, 6.0, ((0, 32),))
    values = draw_values(jax.random.fold_in(key_of[4], 71), 0)
    cotangent = draw_cotangent(jax.random.fold_in(key_of[4], 71), 0)
    return dict(queries=queries, keys=keys, values=values, cotangent=cotangent)


def features(x):
    wide = x.astype(jnp.float32)
    return jnp.where(wide > 0, wide + 1.0, jnp.exp(jnp.minimum(wide, 0.0)))


def slope(x):
    wide = x.astype(jnp.float32)
    return jnp.where(wide > 0, 1.0, jnp.exp(jnp.minimum(wide, 0.0)))


def reference(queries, keys, values, cotangent):
    blocks = TOKENS // TOK_DEV
    shaped = (blocks, TOK_DEV, HEADS, HD)
    query_blocks = queries.reshape(shaped)
    key_blocks = keys.reshape(shaped)
    value_blocks = values.reshape(shaped)
    cotan_blocks = cotangent.reshape(shaped)
    rows = lax.broadcasted_iota(jnp.int32, (TOK_DEV, TOK_DEV), 0)
    cols = lax.broadcasted_iota(jnp.int32, (TOK_DEV, TOK_DEV), 1)
    causal = (cols <= rows)[None]
    highest = lax.Precision.HIGHEST

    def forward_block(carry, inputs):
        state, normal = carry
        query_rows, key_rows, value_rows, cotan_rows = inputs
        q_feat = features(query_rows).astype(jnp.bfloat16).astype(jnp.float32)
        k_feat = features(key_rows).astype(jnp.bfloat16).astype(jnp.float32)
        value_wide = value_rows.astype(jnp.float32)
        scores = jnp.einsum('thd,shd->hts', q_feat, k_feat)
        scores = jnp.where(causal, scores, 0.0)
        weights = scores.astype(jnp.bfloat16).astype(jnp.float32)
        state_low = state.astype(jnp.bfloat16).astype(jnp.float32)
        den = jnp.sum(scores, axis=2).T + jnp.einsum('thd,hd->th', q_feat, normal, precision=highest)
        num = jnp.einsum('hts,she->the', weights, value_wide) + jnp.einsum('thd,hde->the', q_feat, state_low)
        ratio = num / den[:, :, None]
        cotan_wide = cotan_rows.astype(jnp.float32)
        grad_scaled = (cotan_wide / den[:, :, None]).astype(jnp.bfloat16).astype(jnp.float32)
        grad_den = -jnp.sum(cotan_wide * ratio, axis=2) / den
        grad_scores = jnp.einsum('the,she->hts', grad_scaled, value_wide) + grad_den.T[:, :, None]
        grad_scores = jnp.where(causal, grad_scores, 0.0).astype(jnp.bfloat16).astype(jnp.float32)
        q_lin = jnp.einsum('hts,shd->thd', grad_scores, k_feat) + jnp.einsum('the,hde->thd', grad_scaled, state_low)
        q_lin = q_lin + grad_den[:, :, None] * normal[None]
        query_grad = (q_lin * slope(query_rows)).astype(jnp.bfloat16)
        new_state = state + jnp.einsum('shd,she->hde', k_feat, value_wide)
        new_normal = normal + jnp.sum(k_feat, axis=0)
        return (new_state, new_normal), (ratio.astype(jnp.bfloat16), query_grad, grad_scaled, grad_den)

    start = (jnp.zeros((HEADS, HD, HD), jnp.float32), jnp.zeros((HEADS, HD), jnp.float32))
    _, (attended, query_grad, grad_all, grad_den_all) = lax.scan(
        forward_block, start, (query_blocks, key_blocks, value_blocks, cotan_blocks))

    def backward_block(carry, inputs):
        later, later_norm = carry
        query_rows, key_rows, value_rows, grad_scaled, grad_den = inputs
        q_feat = features(query_rows).astype(jnp.bfloat16).astype(jnp.float32)
        k_feat = features(key_rows).astype(jnp.bfloat16).astype(jnp.float32)
        value_wide = value_rows.astype(jnp.float32)
        scores = jnp.where(causal, jnp.einsum('thd,shd->hts', q_feat, k_feat), 0.0)
        weights = scores.astype(jnp.bfloat16).astype(jnp.float32)
        grad_scores = jnp.einsum('the,she->hts', grad_scaled, value_wide) + grad_den.T[:, :, None]
        grad_scores = jnp.where(causal, grad_scores, 0.0).astype(jnp.bfloat16).astype(jnp.float32)
        later_low = later.astype(jnp.bfloat16).astype(jnp.float32)
        k_lin = jnp.einsum('hts,thd->shd', grad_scores, q_feat) + jnp.einsum('she,hde->shd', value_wide, later_low)
        k_lin = k_lin + later_norm[None]
        key_grad = (k_lin * slope(key_rows)).astype(jnp.bfloat16)
        value_grad = jnp.einsum('hts,the->she', weights, grad_scaled) + jnp.einsum('shd,hde->she', k_feat, later_low)
        new_later = later + jnp.einsum('thd,the->hde', q_feat, grad_scaled)
        new_norm = later_norm + jnp.einsum('th,thd->hd', grad_den, q_feat, precision=highest)
        return (new_later, new_norm), (key_grad, value_grad.astype(jnp.bfloat16))

    _, (key_grad, value_grad) = lax.scan(
        backward_block, start, (query_blocks, key_blocks, value_blocks, grad_all, grad_den_all), reverse=True)
    flat = (TOKENS, HEADS * HD)
    return (attended.reshape(flat), query_grad.reshape(flat), key_grad.reshape(flat), value_grad.reshape(flat))
```

```python
import functools

import jax
import jax.numpy as jnp
from jax import lax
from jax.experimental import pallas as pl
from jax.experimental.pallas import tpu as pltpu
from jax.sharding import PartitionSpec as P

HD = 128
F32 = jnp.float32
BF16 = jnp.bfloat16


def features(wide):
    return jnp.where(wide > 0, wide + 1.0, jnp.exp(jnp.minimum(wide, 0.0))).astype(BF16)


def slope(wide):
    return jnp.where(wide > 0, 1.0, jnp.exp(jnp.minimum(wide, 0.0)))


def dot(a, b, contract):
    return lax.dot_general(a, b, (contract, ((), ())), preferred_element_type=F32)


NN = ((1,), (0,))
NT = ((1,), (1,))
TN = ((0,), (0,))


def columns(head):
    return slice(head * HD, (head + 1) * HD)


def causal(count):
    rows = lax.broadcasted_iota(jnp.int32, (count, count), 0)
    cols = lax.broadcasted_iota(jnp.int32, (count, count), 1)
    return cols <= rows


def state_kernel(k_ref, v_ref, state_ref, norm_ref):
    for h in range(k_ref.shape[1] // HD):
        at = columns(h)
        k_feat = features(k_ref[:, at].astype(F32))
        state_ref[at, :] = dot(k_feat, v_ref[:, at], TN)
        norm_ref[h : h + 1, :] = jnp.sum(k_feat.astype(F32), axis=0, keepdims=True)


def later_kernel(q_ref, k_ref, c_ref, norm_ref, later_ref, scaled_ref, den_ref):
    mask = causal(q_ref.shape[0])
    for h in range(q_ref.shape[1] // HD):
        at = columns(h)
        q_feat = features(q_ref[:, at].astype(F32))
        k_feat = features(k_ref[:, at].astype(F32))
        scores = jnp.where(mask, dot(q_feat, k_feat, NT), 0.0)
        den = jnp.sum(scores + q_feat.astype(F32) * norm_ref[h : h + 1, :], axis=1, keepdims=True)
        scaled = (c_ref[:, at].astype(F32) / den).astype(BF16)
        den_ref[:, h : h + 1] = den
        scaled_ref[:, at] = scaled
        later_ref[at, :] = dot(q_feat, scaled, TN)


def query_kernel(
    q_ref, k_ref, v_ref, c_ref, scaled_ref, den_ref, norm_ref, state_ref,
    att_ref, qg_ref, ki_ref, vi_ref, lnorm_ref,
):
    mask = causal(q_ref.shape[0])
    for h in range(q_ref.shape[1] // HD):
        at = columns(h)
        q_wide = q_ref[:, at].astype(F32)
        q_feat = features(q_wide)
        k_feat = features(k_ref[:, at].astype(F32))
        value = v_ref[:, at]
        scaled = scaled_ref[:, at]
        den = den_ref[:, h : h + 1]
        state_low = state_ref[at, :].astype(BF16)
        scores = jnp.where(mask, dot(q_feat, k_feat, NT), 0.0)
        weights = scores.astype(BF16)
        num = dot(weights, value, NN) + dot(q_feat, state_low, NN)
        ratio = num / den
        att_ref[:, at] = ratio.astype(BF16)
        grad_den = -jnp.sum(c_ref[:, at].astype(F32) * ratio, axis=1, keepdims=True) / den
        grad_scores = dot(scaled, value, NT) + grad_den
        grad_scores = jnp.where(mask, grad_scores, 0.0).astype(BF16)
        q_lin = dot(grad_scores, k_feat, NN) + dot(scaled, state_low, NT)
        q_lin = q_lin + grad_den * norm_ref[h : h + 1, :]
        qg_ref[:, at] = (q_lin * slope(q_wide)).astype(BF16)
        lnorm_ref[h : h + 1, :] = jnp.sum(grad_den * q_feat.astype(F32), axis=0, keepdims=True)
        ki_ref[:, at] = dot(grad_scores, q_feat, TN)
        vi_ref[:, at] = dot(weights, scaled, TN)


def key_kernel(k_ref, v_ref, ki_ref, vi_ref, lnorm_ref, later_ref, kg_ref, vg_ref):
    for h in range(k_ref.shape[1] // HD):
        at = columns(h)
        k_wide = k_ref[:, at].astype(F32)
        later_low = later_ref[at, :].astype(BF16)
        k_lin = ki_ref[:, at] + dot(v_ref[:, at], later_low, NT) + lnorm_ref[h : h + 1, :]
        kg_ref[:, at] = (k_lin * slope(k_wide)).astype(BF16)
        vg_ref[:, at] = (vi_ref[:, at] + dot(features(k_wide), later_low, NN)).astype(BF16)


def call(kernel, outs, *args):
    flops = 2 * HD * HD * HD * 16
    return pl.pallas_call(
        kernel,
        out_shape=[jax.ShapeDtypeStruct(shape, kind) for shape, kind in outs],
        compiler_params=pltpu.CompilerParams(vmem_limit_bytes=48 * 1024 * 1024),
        cost_estimate=pl.CostEstimate(flops=flops, bytes_accessed=4 << 20, transcendentals=0),
    )(*args)


def bits(axis):
    return (lax.axis_size(axis) - 1).bit_length()


def swap(part, axis, bit):
    return lax.ppermute(part, axis, [(i, i ^ (1 << bit)) for i in range(lax.axis_size(axis))])


def is_late(axis, bit, backward):
    set_bit = (lax.axis_index(axis) >> bit) & 1
    return set_bit == (0 if backward else 1)


def scan_small(part, backward):
    before = jnp.zeros_like(part)
    levels = [("inner", b) for b in range(bits("inner"))] + [("outer", b) for b in range(bits("outer"))]
    for axis, bit in levels:
        got = swap(part, axis, bit)
        before = before + jnp.where(is_late(axis, bit, backward), got, 0.0)
        part = part + got
    return before


def scan_large(part, backward):
    halving = [("inner", b) for b in range(bits("inner"))] + [("outer", 0)]
    doubling = [("outer", b) for b in range(1, bits("outer"))]
    lows = []
    for axis, bit in halving:
        late = is_late(axis, bit, backward)
        half = part.shape[0] // 2
        first, second = part[:half], part[half:]
        mine = jnp.where(late, second, first)
        got = swap(jnp.where(late, first, second), axis, bit)
        lows.append(jnp.where(late, got, mine))
        part = mine + got
    before = jnp.zeros_like(part)
    for axis, bit in doubling:
        got = swap(part, axis, bit)
        before = before + jnp.where(is_late(axis, bit, backward), got, 0.0)
        part = part + got
    for (axis, bit), low in zip(reversed(halving), reversed(lows)):
        late = is_late(axis, bit, backward)
        both = before + low
        mine = jnp.where(late, both, before)
        got = swap(jnp.where(late, before, both), axis, bit)
        first = jnp.where(late, got, mine)
        second = jnp.where(late, mine, got)
        before = jnp.concatenate([first, second])
    return before


def scan_chunks(part, backward, chunks):
    size = part.shape[0] // chunks
    return jnp.concatenate([scan_large(part[i * size : (i + 1) * size], backward) for i in range(chunks)])


def per_device(queries, keys, values, cotangent):
    tokens, width = queries.shape
    heads = width // HD
    flat, square, small = (tokens, width), (width, HD), (heads, HD)
    local_state, local_norm = call(state_kernel, [(square, F32), (small, F32)], keys, values)
    normal = scan_small(local_norm, False)
    state = scan_chunks(local_state, False, 2)
    later_local, scaled, den = call(
        later_kernel, [(square, F32), (flat, BF16), ((tokens, HD), F32)], queries, keys, cotangent, normal
    )
    later = scan_chunks(later_local, True, 2)
    attended, query_grad, k_intra, v_intra, local_lnorm = call(
        query_kernel,
        [(flat, BF16), (flat, BF16), (flat, F32), (flat, F32), (small, F32)],
        queries, keys, values, cotangent, scaled, den, normal, state,
    )
    later_norm = scan_small(local_lnorm, True)
    key_grad, value_grad = call(
        key_kernel, [(flat, BF16), (flat, BF16)], keys, values, k_intra, v_intra, later_norm, later
    )
    return attended, query_grad, key_grad, value_grad


def solution(mesh):
    rows = P(("outer", "inner"), None)
    return jax.shard_map(
        per_device, mesh=mesh, in_specs=(rows,) * 4, out_specs=(rows,) * 4, check_vma=False
    )
```

```python
import functools

import jax
import jax.numpy as jnp
from jax import lax
from jax.experimental import pallas as pl
from jax.experimental.pallas import tpu as pltpu
from jax.sharding import PartitionSpec as P

HD = 128
F32 = jnp.float32
BF16 = jnp.bfloat16


def features(wide):
    return jnp.where(wide > 0, wide + 1.0, jnp.exp(jnp.minimum(wide, 0.0))).astype(BF16)


def slope(wide):
    return jnp.where(wide > 0, 1.0, jnp.exp(jnp.minimum(wide, 0.0)))


def dot(a, b, contract):
    return lax.dot_general(a, b, (contract, ((), ())), preferred_element_type=F32)


NN = ((1,), (0,))
NT = ((1,), (1,))
TN = ((0,), (0,))


def columns(head):
    return slice(head * HD, (head + 1) * HD)


def causal(count, key_axis):
    keys = lax.broadcasted_iota(jnp.int32, (count, count), key_axis)
    queries = lax.broadcasted_iota(jnp.int32, (count, count), 1 - key_axis)
    return keys <= queries


def parts(row):
    high = row.astype(BF16)
    rest = row - high.astype(F32)
    middle = rest.astype(BF16)
    low = (rest - middle.astype(F32)).astype(BF16)
    return jnp.concatenate([high, middle, low], axis=0)


def row_dot(row, matrix):
    return jnp.sum(dot(parts(row), matrix, NN), axis=0, keepdims=True)


def state_kernel(k_ref, v_ref, state_ref, norm_ref):
    for h in range(k_ref.shape[1] // HD):
        at = columns(h)
        k_feat = features(k_ref[:, at].astype(F32))
        state_ref[at, :] = dot(k_feat, v_ref[:, at], TN)
        norm_ref[h : h + 1, :] = jnp.sum(k_feat.astype(F32), axis=0, keepdims=True)


def weights_kernel(q_ref, k_ref, c_ref, qf_ref, kf_ref, qt_ref, ct_ref, w_ref, part_ref):
    mask = causal(q_ref.shape[0], 0)
    for h in range(q_ref.shape[1] // HD):
        at = columns(h)
        q_feat = features(q_ref[:, at].astype(F32))
        k_feat = features(k_ref[:, at].astype(F32))
        scores = jnp.where(mask, dot(k_feat, q_feat, NT), 0.0)
        qf_ref[:, at] = q_feat
        kf_ref[:, at] = k_feat
        qt_ref[at, :] = q_feat.T
        ct_ref[at, :] = c_ref[:, at].T
        w_ref[:, at] = scores.astype(BF16)
        part_ref[h : h + 1, :] = jnp.sum(scores, axis=0, keepdims=True)


def later_kernel(qt_ref, ct_ref, part_ref, norm_ref, later_ref, scaled_ref, inv_ref):
    for h in range(part_ref.shape[0]):
        at = columns(h)
        row = slice(h, h + 1)
        q_turned = qt_ref[at, :]
        inverse = 1.0 / (part_ref[row, :] + row_dot(norm_ref[row, :], q_turned))
        scaled = (ct_ref[at, :].astype(F32) * inverse).astype(BF16)
        inv_ref[row, :] = inverse
        scaled_ref[at, :] = scaled
        later_ref[at, :] = dot(q_turned, scaled, NT)


def near_kernel(w_ref, scaled_ref, v_ref, num_ref, gs_ref, vi_ref, plain_ref):
    for h in range(w_ref.shape[1] // HD):
        at = columns(h)
        weights, value = w_ref[:, at], v_ref[:, at]
        scaled = scaled_ref[at, :].T
        plain_ref[:, at] = scaled
        num_ref[at, :] = dot(value, weights, TN)
        gs_ref[:, at] = dot(scaled, value, NT)
        vi_ref[:, at] = dot(weights, scaled, NN)


def attend_kernel(qf_ref, qt_ref, ct_ref, inv_ref, num_ref, state_ref, ratio_ref, gden_ref, lnorm_ref):
    for h in range(inv_ref.shape[0]):
        at = columns(h)
        row = slice(h, h + 1)
        inverse = inv_ref[row, :]
        ratio = (num_ref[at, :] + dot(state_ref[at, :].astype(BF16), qt_ref[at, :], TN)) * inverse
        ratio_ref[at, :] = ratio.astype(BF16)
        grad_den = -jnp.sum(ct_ref[at, :].astype(F32) * ratio, axis=0, keepdims=True) * inverse
        gden_ref[row, :] = grad_den
        lnorm_ref[row, :] = row_dot(grad_den, qf_ref[:, at])


def query_kernel(
    q_ref, qf_ref, kf_ref, scaled_ref, ratio_ref, gden_ref, norm_ref, gs_ref, state_ref, att_ref, qg_ref, ki_ref
):
    mask = causal(q_ref.shape[0], 1)
    gden_columns = gden_ref[...].T
    for h in range(gden_ref.shape[0]):
        at = columns(h)
        grad_den = gden_columns[:, h : h + 1]
        grad_scores = jnp.where(mask, gs_ref[:, at] + grad_den, 0.0).astype(BF16)
        q_lin = dot(grad_scores, kf_ref[:, at], NN) + dot(scaled_ref[:, at], state_ref[at, :].astype(BF16), NT)
        q_lin = q_lin + grad_den * norm_ref[h : h + 1, :]
        qg_ref[:, at] = (q_lin * slope(q_ref[:, at].astype(F32))).astype(BF16)
        ki_ref[:, at] = dot(grad_scores, qf_ref[:, at], TN)
        att_ref[:, at] = ratio_ref[at, :].T


def key_kernel(k_ref, kf_ref, v_ref, ki_ref, vi_ref, lnorm_ref, later_ref, kg_ref, vg_ref):
    for h in range(k_ref.shape[1] // HD):
        at = columns(h)
        later_low = later_ref[at, :].astype(BF16)
        k_lin = ki_ref[:, at] + dot(v_ref[:, at], later_low, NT) + lnorm_ref[h : h + 1, :]
        kg_ref[:, at] = (k_lin * slope(k_ref[:, at].astype(F32))).astype(BF16)
        vg_ref[:, at] = (vi_ref[:, at] + dot(kf_ref[:, at], later_low, NN)).astype(BF16)


COST = dict(state=1.0, weights=1.0, later=1.0, near=1.0, attend=1.0, query=1.0, key=1.0)
CHUNKS = (2, 2)
RADIX = 2
EARLY = ("N", "S0<N", "S1<N", "N", "N", "N")
GATE = "S0"
LATE = ()
LAST = ()
VMEM = 16


def call(name, kernel, outs, *args):
    return pl.pallas_call(
        kernel,
        out_shape=[jax.ShapeDtypeStruct(shape, kind) for shape, kind in outs],
        compiler_params=pltpu.CompilerParams(vmem_limit_bytes=VMEM << 20),
        cost_estimate=pl.CostEstimate(flops=0, bytes_accessed=int(COST[name] * 3.5e6), transcendentals=0),
        name=name,
    )(*args)


def bits(axis):
    return (lax.axis_size(axis) - 1).bit_length()


def swap(part, axis, mask):
    return lax.ppermute(part, axis, [(i, i ^ mask) for i in range(lax.axis_size(axis))])


def is_late(axis, mask, backward):
    set_bit = (lax.axis_index(axis) >> (mask.bit_length() - 1)) & 1
    return set_bit == (0 if backward else 1)


def groups(axis, start, radix):
    spans = [(b, min(b + radix, bits(axis))) for b in range(start, bits(axis), radix)]
    return [(axis, [m << low for m in range(1, 1 << (high - low))]) for low, high in spans]


def tie(value, others):
    return lax.optimization_barrier((value, *others))[0] if others else value


def add_up(part, levels, backward):
    before = jnp.zeros_like(part)
    for axis, masks in levels:
        got = yield [(part, axis, mask) for mask in masks]
        for mask, other in zip(masks, got):
            before = before + jnp.where(is_late(axis, mask, backward), other, 0.0)
            part = part + other
    return before


def scan_small(part, backward):
    levels = groups("inner", 0, RADIX) + [("outer", [1])] + groups("outer", 1, RADIX)
    return add_up(part, levels, backward)


def scan_large(part, backward):
    halving = [("inner", 1 << b) for b in range(bits("inner"))] + [("outer", 1)]
    lows = []
    for axis, mask in halving:
        late = is_late(axis, mask, backward)
        half = part.shape[0] // 2
        first, second = part[:half], part[half:]
        mine = jnp.where(late, second, first)
        (got,) = yield [(jnp.where(late, first, second), axis, mask)]
        lows.append(jnp.where(late, got, mine))
        part = mine + got
    before = yield from add_up(part, groups("outer", 1, RADIX), backward)
    for (axis, mask), low in zip(reversed(halving), reversed(lows)):
        late = is_late(axis, mask, backward)
        both = before + low
        mine = jnp.where(late, both, before)
        (got,) = yield [(jnp.where(late, before, both), axis, mask)]
        first = jnp.where(late, got, mine)
        second = jnp.where(late, mine, got)
        before = jnp.concatenate([first, second])
    return before


class Chain:
    def __init__(self, scan):
        self.scan = scan
        self.arrived = []
        self.result = None
        self.ask = next(scan)

    def hop(self, after=()):
        got = [swap(tie(part, after), axis, mask) for part, axis, mask in self.ask]
        self.arrived.append(got)
        try:
            self.ask = self.scan.send(got)
        except StopIteration as end:
            self.ask, self.result = None, end.value


def split(part, chunks, backward):
    size = part.shape[0] // chunks
    return [Chain(scan_large(part[i * size : (i + 1) * size], backward)) for i in range(chunks)]


def last(chains, names):
    found = []
    for name, _, hop in (entry.partition(".") for entry in names.split(",")):
        if name in chains and chains[name].arrived:
            arrived = chains[name].arrived
            found.extend(arrived[min(int(hop), len(arrived) - 1)] if hop else arrived[-1])
    return found


def run(chains, order):
    for entry in order:
        name, _, others = entry.partition("<")
        if name in chains and chains[name].ask:
            chains[name].hop(last(chains, others))


def drain(chains, kind):
    ours = [chains[name] for name in sorted(chains) if name[0] == kind]
    while any(chain.ask for chain in ours):
        for chain in ours:
            if chain.ask:
                chain.hop()
    results = [chain.result for chain in ours]
    return jnp.concatenate(results) if len(results) > 1 else results[0]


def per_device(queries, keys, values, cotangent):
    tokens, width = queries.shape
    heads = width // HD
    flat, turned, square, pairs = (tokens, width), (width, tokens), (width, HD), (tokens, heads * tokens)
    small, column = (heads, HD), (heads, tokens)
    local_state, local_norm = call("state", state_kernel, [(square, F32), (small, F32)], keys, values)
    chains = {"N": Chain(scan_small(local_norm, False))}
    chains.update(("S%d" % i, chain) for i, chain in enumerate(split(local_state, CHUNKS[0], False)))
    run(chains, EARLY)
    normal = tie(drain(chains, "N"), last(chains, GATE))
    q_feat, k_feat, q_turned, c_turned, weights, part = call(
        "weights", weights_kernel,
        [(flat, BF16), (flat, BF16), (turned, BF16), (turned, BF16), (pairs, BF16), (column, F32)],
        queries, keys, cotangent,
    )
    later_local, scaled, inverse = call(
        "later", later_kernel, [(square, F32), (turned, BF16), (column, F32)], q_turned, c_turned, part, normal
    )
    chains.update(("L%d" % i, chain) for i, chain in enumerate(split(later_local, CHUNKS[1], True)))
    run(chains, LATE)
    state = drain(chains, "S")
    near_num, near_scores, near_values, plain = call(
        "near", near_kernel, [(turned, F32), (pairs, F32), (flat, F32), (flat, BF16)], weights, scaled, values
    )
    ratio, grad_den, local_lnorm = call(
        "attend", attend_kernel, [(turned, BF16), (column, F32), (small, F32)],
        q_feat, q_turned, c_turned, inverse, near_num, state,
    )
    chains["M"] = Chain(scan_small(local_lnorm, True))
    run(chains, LAST)
    later_norm = drain(chains, "M")
    later = drain(chains, "L")
    attended, query_grad, near_keys = call(
        "query", query_kernel, [(flat, BF16), (flat, BF16), (flat, F32)],
        queries, q_feat, k_feat, plain, ratio, grad_den, normal, near_scores, state,
    )
    key_grad, value_grad = call(
        "key", key_kernel, [(flat, BF16), (flat, BF16)],
        keys, k_feat, values, near_keys, near_values, later_norm, later,
    )
    return attended, query_grad, key_grad, value_grad


def solution(mesh):
    rows = P(("outer", "inner"), None)
    return jax.shard_map(
        per_device, mesh=mesh, in_specs=(rows,) * 4, out_specs=(rows,) * 4, check_vma=False
    )
```

```python
import functools

import jax
import jax.numpy as jnp
from jax import lax
from jax.experimental import pallas as pl
from jax.experimental.pallas import tpu as pltpu
from jax.sharding import PartitionSpec as P

HD = 128
F32 = jnp.float32
BF16 = jnp.bfloat16


def features(wide):
    return jnp.where(wide > 0, wide + 1.0, jnp.exp(jnp.minimum(wide, 0.0))).astype(BF16)


def slope(wide):
    return jnp.where(wide > 0, 1.0, jnp.exp(jnp.minimum(wide, 0.0)))


def dot(a, b, contract):
    return lax.dot_general(a, b, (contract, ((), ())), preferred_element_type=F32)


NN = ((1,), (0,))
NT = ((1,), (1,))
TN = ((0,), (0,))


def columns(head):
    return slice(head * HD, (head + 1) * HD)


def causal(count, key_axis):
    keys = lax.broadcasted_iota(jnp.int32, (count, count), key_axis)
    queries = lax.broadcasted_iota(jnp.int32, (count, count), 1 - key_axis)
    return keys <= queries


def parts(row):
    high = row.astype(BF16)
    rest = row - high.astype(F32)
    middle = rest.astype(BF16)
    low = (rest - middle.astype(F32)).astype(BF16)
    return jnp.concatenate([high, middle, low], axis=0)


def row_dot(row, matrix):
    return jnp.sum(dot(parts(row), matrix, NN), axis=0, keepdims=True)


def state_kernel(k_hbm, v_hbm, state_ref, norm_ref, k_ref, v_ref, sems):
    copies = [
        pltpu.make_async_copy(k_hbm, k_ref, sems.at[0]),
        pltpu.make_async_copy(v_hbm, v_ref, sems.at[1]),
    ]
    for copy in copies:
        copy.start()
    for copy in copies:
        copy.wait()
    for h in range(k_ref.shape[1] // HD):
        at = columns(h)
        k_feat = features(k_ref[:, at].astype(F32))
        state_ref[at, :] = dot(k_feat, v_ref[:, at], TN)
        norm_ref[h : h + 1, :] = jnp.sum(k_feat.astype(F32), axis=0, keepdims=True)


def weights_kernel(q_ref, k_ref, c_ref, qf_ref, kf_ref, qt_ref, ct_ref, w_ref, part_ref):
    mask = causal(q_ref.shape[0], 0)
    for h in range(q_ref.shape[1] // HD):
        at = columns(h)
        q_feat = features(q_ref[:, at].astype(F32))
        k_feat = features(k_ref[:, at].astype(F32))
        scores = jnp.where(mask, dot(k_feat, q_feat, NT), 0.0)
        qf_ref[:, at] = q_feat
        kf_ref[:, at] = k_feat
        qt_ref[at, :] = q_feat.T
        ct_ref[at, :] = c_ref[:, at].T
        w_ref[:, at] = scores.astype(BF16)
        part_ref[h : h + 1, :] = jnp.sum(scores, axis=0, keepdims=True)


def later_kernel(qt_ref, ct_ref, part_ref, norm_ref, later_ref, scaled_ref, inv_ref):
    for h in range(part_ref.shape[0]):
        at = columns(h)
        row = slice(h, h + 1)
        q_turned = qt_ref[at, :]
        inverse = 1.0 / (part_ref[row, :] + row_dot(norm_ref[row, :], q_turned))
        scaled = (ct_ref[at, :].astype(F32) * inverse).astype(BF16)
        inv_ref[row, :] = inverse
        scaled_ref[at, :] = scaled
        later_ref[at, :] = dot(q_turned, scaled, NT)


def near_kernel(w_ref, scaled_ref, v_ref, num_ref, gs_ref, vi_ref, plain_ref):
    for h in range(w_ref.shape[1] // HD):
        at = columns(h)
        weights, value = w_ref[:, at], v_ref[:, at]
        scaled = scaled_ref[at, :].T
        plain_ref[:, at] = scaled
        num_ref[at, :] = dot(value, weights, TN)
        gs_ref[:, at] = dot(scaled, value, NT)
        vi_ref[:, at] = dot(weights, scaled, NN)


def attend_kernel(qf_ref, qt_ref, ct_ref, inv_ref, num_ref, state_ref, ratio_ref, gden_ref, lnorm_ref):
    for h in range(inv_ref.shape[0]):
        at = columns(h)
        row = slice(h, h + 1)
        inverse = inv_ref[row, :]
        ratio = (num_ref[at, :] + dot(state_ref[at, :].astype(BF16), qt_ref[at, :], TN)) * inverse
        ratio_ref[at, :] = ratio.astype(BF16)
        grad_den = -jnp.sum(ct_ref[at, :].astype(F32) * ratio, axis=0, keepdims=True) * inverse
        gden_ref[row, :] = grad_den
        lnorm_ref[row, :] = row_dot(grad_den, qf_ref[:, at])


def query_kernel(
    q_ref, qf_ref, kf_ref, scaled_ref, ratio_ref, gden_ref, norm_ref, gs_ref, state_ref, att_ref, qg_ref, ki_ref
):
    mask = causal(q_ref.shape[0], 1)
    gden_columns = gden_ref[...].T
    for h in range(gden_ref.shape[0]):
        at = columns(h)
        grad_den = gden_columns[:, h : h + 1]
        grad_scores = jnp.where(mask, gs_ref[:, at] + grad_den, 0.0).astype(BF16)
        q_lin = dot(grad_scores, kf_ref[:, at], NN) + dot(scaled_ref[:, at], state_ref[at, :].astype(BF16), NT)
        q_lin = q_lin + grad_den * norm_ref[h : h + 1, :]
        qg_ref[:, at] = (q_lin * slope(q_ref[:, at].astype(F32))).astype(BF16)
        ki_ref[:, at] = dot(grad_scores, qf_ref[:, at], TN)
        att_ref[:, at] = ratio_ref[at, :].T


def key_kernel(k_ref, kf_ref, v_ref, ki_ref, vi_ref, lnorm_ref, later_ref, kg_ref, vg_ref):
    for h in range(k_ref.shape[1] // HD):
        at = columns(h)
        later_low = later_ref[at, :].astype(BF16)
        k_lin = ki_ref[:, at] + dot(v_ref[:, at], later_low, NT) + lnorm_ref[h : h + 1, :]
        kg_ref[:, at] = (k_lin * slope(k_ref[:, at].astype(F32))).astype(BF16)
        vg_ref[:, at] = (vi_ref[:, at] + dot(kf_ref[:, at], later_low, NN)).astype(BF16)


COST = dict(state=1.0, weights=1.0, later=1.0, near=1.0, attend=1.0, query=1.0, key=1.0)
CHUNKS = ((2, 0), (2, 0))
RADIX = 2
INNER_FIRST = (True, True)
PIECE = 256
EARLY = ('S0', 'N', 'N', 'N<S0')
GATE = "S0.0.0"
NEAR_GATE = ""
QUERY_GATE = "L0.5"
LATE = ('S0', 'L0', 'S0', 'L0', 'S0', 'L0', 'S0', 'L0', 'S0', 'L0', 'S0', 'L0')
LAST = ('M', 'M', 'M', 'L0')
VMEM = 16


def call(name, kernel, outs, *args, **more):
    return pl.pallas_call(
        kernel,
        out_shape=[jax.ShapeDtypeStruct(shape, kind) for shape, kind in outs],
        compiler_params=pltpu.CompilerParams(vmem_limit_bytes=VMEM << 20),
        cost_estimate=pl.CostEstimate(flops=0, bytes_accessed=int(COST[name] * 3.5e6), transcendentals=0),
        name=name,
        **more,
    )(*args)


def bits(axis):
    return (lax.axis_size(axis) - 1).bit_length()


def swap(part, axis, mask):
    route = [(i, i ^ mask) for i in range(lax.axis_size(axis))]
    pieces = [part[at : at + PIECE] for at in range(0, part.shape[0], PIECE)]
    got = [lax.ppermute(piece, axis, route) for piece in pieces]
    return jnp.concatenate(got) if len(got) > 1 else got[0]


def is_late(axis, mask, backward):
    set_bit = (lax.axis_index(axis) >> (mask.bit_length() - 1)) & 1
    return set_bit == (0 if backward else 1)


def groups(axis, start, radix):
    spans = [(b, min(b + radix, bits(axis))) for b in range(start, bits(axis), radix)]
    return [(axis, [m << low for m in range(1, 1 << (high - low))]) for low, high in spans]


def tie(value, others):
    return lax.optimization_barrier((value, *others))[0] if others else value


def add_up(part, levels, backward):
    before = jnp.zeros_like(part)
    for axis, masks in levels:
        got = yield [(part, axis, mask) for mask in masks]
        for mask, other in zip(masks, got):
            before = before + jnp.where(is_late(axis, mask, backward), other, 0.0)
            part = part + other
    return before


def scan_small(part, backward, inner_first):
    if inner_first:
        levels = groups("inner", 0, RADIX) + [("outer", [1])] + groups("outer", 1, RADIX)
        return (yield from add_up(part, levels, backward))
    before = yield from add_up(part, [("outer", [1])] + groups("outer", 1, RADIX), backward)
    rows = part.shape[0]
    upto, result = before + part, before
    for axis, masks in groups("inner", 0, RADIX):
        both = jnp.concatenate([before, upto])
        got = yield [(both, axis, mask) for mask in masks]
        for mask, other in zip(masks, got):
            result = result + jnp.where(is_late(axis, mask, backward), other[rows:], other[:rows])
            before, upto = before + other[:rows], upto + other[rows:]
    return result


def scan_large(part, backward, chunks, joined):
    size = part.shape[0] // chunks
    parts = [part[i * size : (i + 1) * size] for i in range(chunks)]
    halving = [("inner", 1 << b) for b in range(bits("inner"))] + [("outer", 1)]
    lows = []
    for step, (axis, mask) in enumerate(halving):
        if axis == "outer":
            parts = [jnp.concatenate(parts)]
        late = is_late(axis, mask, backward)
        half = parts[0].shape[0] // 2
        sends = [jnp.where(late, part[:half], part[half:]) for part in parts]
        if step < joined:
            sends = [jnp.concatenate(sends)]
        got = yield [(send, axis, mask) for send in sends]
        if len(got) < len(parts):
            got = [got[0][i * half : (i + 1) * half] for i in range(len(parts))]
        mine = [jnp.where(late, part[half:], part[:half]) for part in parts]
        lows.append([jnp.where(late, other, own) for other, own in zip(got, mine)])
        parts = [own + other for own, other in zip(mine, got)]
    befores = [(yield from add_up(parts[0], groups("outer", 1, RADIX), backward))]
    for (axis, mask), low in zip(reversed(halving), reversed(lows)):
        if len(low) > len(befores):
            size = befores[0].shape[0] // chunks
            befores = [befores[0][i * size : (i + 1) * size] for i in range(chunks)]
        late = is_late(axis, mask, backward)
        both = [before + other for before, other in zip(befores, low)]
        got = yield [(jnp.where(late, before, full), axis, mask) for before, full in zip(befores, both)]
        mine = [jnp.where(late, full, before) for before, full in zip(befores, both)]
        befores = [
            jnp.concatenate([jnp.where(late, other, own), jnp.where(late, own, other)])
            for other, own in zip(got, mine)
        ]
    return jnp.concatenate(befores)


class Chain:
    def __init__(self, scan):
        self.scan = scan
        self.arrived = []
        self.result = None
        self.ask = next(scan)

    def hop(self, after=()):
        got = [swap(tie(part, after), axis, mask) for part, axis, mask in self.ask]
        self.arrived.append(got)
        try:
            self.ask = self.scan.send(got)
        except StopIteration as end:
            self.ask, self.result = None, end.value


def split(part, chunks, backward):
    return [Chain(scan_large(part, backward, *chunks))]


def last(chains, names):
    found = []
    for name, *place in (entry.split(".") for entry in names.split(",")):
        if name in chains and chains[name].arrived:
            arrived = chains[name].arrived
            got = arrived[min(int(place[0]), len(arrived) - 1)] if place else arrived[-1]
            found.extend(got[int(place[1]) % len(got) :][:1] if place[1:] else got)
    return found


def run(chains, order):
    for entry in order:
        name, _, others = entry.partition("<")
        if name in chains and chains[name].ask:
            chains[name].hop(last(chains, others))


def drain(chains, kind):
    ours = [chains[name] for name in sorted(chains) if name[0] == kind]
    while any(chain.ask for chain in ours):
        for chain in ours:
            if chain.ask:
                chain.hop()
    results = [chain.result for chain in ours]
    return jnp.concatenate(results) if len(results) > 1 else results[0]


def per_device(queries, keys, values, cotangent):
    tokens, width = queries.shape
    heads = width // HD
    flat, turned, square, pairs = (tokens, width), (width, tokens), (width, HD), (tokens, heads * tokens)
    small, column = (heads, HD), (heads, tokens)
    local_state, local_norm = call(
        "state", state_kernel, [(square, F32), (small, F32)], keys, values,
        in_specs=[pl.BlockSpec(memory_space=pltpu.HBM)] * 2,
        scratch_shapes=[pltpu.VMEM(flat, BF16), pltpu.VMEM(flat, BF16), pltpu.SemaphoreType.DMA((2,))],
    )
    chains = {"N": Chain(scan_small(local_norm, False, INNER_FIRST[0]))}
    chains.update(("S%d" % i, chain) for i, chain in enumerate(split(local_state, CHUNKS[0], False)))
    run(chains, EARLY)
    normal = tie(drain(chains, "N"), last(chains, GATE))
    q_feat, k_feat, q_turned, c_turned, weights, part = call(
        "weights", weights_kernel,
        [(flat, BF16), (flat, BF16), (turned, BF16), (turned, BF16), (pairs, BF16), (column, F32)],
        queries, keys, cotangent,
    )
    later_local, scaled, inverse = call(
        "later", later_kernel, [(square, F32), (turned, BF16), (column, F32)], q_turned, c_turned, part, normal
    )
    chains.update(("L%d" % i, chain) for i, chain in enumerate(split(later_local, CHUNKS[1], True)))
    run(chains, LATE)
    state = drain(chains, "S")
    near_num, near_scores, near_values, plain = call(
        "near", near_kernel, [(turned, F32), (pairs, F32), (flat, F32), (flat, BF16)], weights, tie(scaled, last(chains, NEAR_GATE)), values
    )
    ratio, grad_den, local_lnorm = call(
        "attend", attend_kernel, [(turned, BF16), (column, F32), (small, F32)],
        q_feat, q_turned, c_turned, inverse, near_num, state,
    )
    chains["M"] = Chain(scan_small(local_lnorm, True, INNER_FIRST[1]))
    run(chains, LAST)
    later_norm = drain(chains, "M")
    later = drain(chains, "L")
    attended, query_grad, near_keys = call(
        "query", query_kernel, [(flat, BF16), (flat, BF16), (flat, F32)],
        queries, q_feat, k_feat, plain, ratio, tie(grad_den, last(chains, QUERY_GATE)), normal, near_scores, state,
    )
    key_grad, value_grad = call(
        "key", key_kernel, [(flat, BF16), (flat, BF16)],
        keys, k_feat, values, near_keys, near_values, later_norm, later,
    )
    return attended, query_grad, key_grad, value_grad


def solution(mesh):
    rows = P(("outer", "inner"), None)
    return jax.shard_map(
        per_device, mesh=mesh, in_specs=(rows,) * 4, out_specs=(rows,) * 4, check_vma=False
    )
```

```python
import functools

import jax
import jax.numpy as jnp
from jax import lax
from jax.experimental import pallas as pl
from jax.experimental.pallas import tpu as pltpu
from jax.sharding import PartitionSpec as P

HD = 128
F32 = jnp.float32
BF16 = jnp.bfloat16


def features(wide):
    return jnp.where(wide > 0, wide + 1.0, jnp.exp(jnp.minimum(wide, 0.0))).astype(BF16)


def slope(wide):
    return jnp.where(wide > 0, 1.0, jnp.exp(jnp.minimum(wide, 0.0)))


def dot(a, b, contract):
    return lax.dot_general(a, b, (contract, ((), ())), preferred_element_type=F32)


NN = ((1,), (0,))
NT = ((1,), (1,))
TN = ((0,), (0,))


def columns(head):
    return slice(head * HD, (head + 1) * HD)


def causal(count, key_axis):
    keys = lax.broadcasted_iota(jnp.int32, (count, count), key_axis)
    queries = lax.broadcasted_iota(jnp.int32, (count, count), 1 - key_axis)
    return keys <= queries


def parts(row):
    high = row.astype(BF16)
    rest = row - high.astype(F32)
    middle = rest.astype(BF16)
    low = (rest - middle.astype(F32)).astype(BF16)
    return jnp.concatenate([high, middle, low], axis=0)


def row_dot(row, matrix):
    return jnp.sum(dot(parts(row), matrix, NN), axis=0, keepdims=True)


def norm_kernel(k_ref, norm_ref):
    for h in range(k_ref.shape[1] // HD):
        k_feat = features(k_ref[:, columns(h)].astype(F32))
        norm_ref[h : h + 1, :] = jnp.sum(k_feat.astype(F32), axis=0, keepdims=True)


def state_kernel(k_ref, v_ref, state_ref):
    for h in range(k_ref.shape[1] // HD):
        at = columns(h)
        state_ref[at, :] = dot(features(k_ref[:, at].astype(F32)), v_ref[:, at], TN)


def weights_kernel(q_ref, k_ref, c_ref, qf_ref, kf_ref, qt_ref, ct_ref, w_ref, part_ref):
    mask = causal(q_ref.shape[0], 0)
    for h in range(q_ref.shape[1] // HD):
        at = columns(h)
        q_feat = features(q_ref[:, at].astype(F32))
        k_feat = features(k_ref[:, at].astype(F32))
        scores = jnp.where(mask, dot(k_feat, q_feat, NT), 0.0)
        qf_ref[:, at] = q_feat
        kf_ref[:, at] = k_feat
        qt_ref[at, :] = q_feat.T
        ct_ref[at, :] = c_ref[:, at].T
        w_ref[:, at] = scores.astype(BF16)
        part_ref[h : h + 1, :] = jnp.sum(scores, axis=0, keepdims=True)


def later_kernel(qt_ref, ct_ref, part_ref, norm_ref, later_ref, scaled_ref, inv_ref):
    for h in range(part_ref.shape[0]):
        at = columns(h)
        row = slice(h, h + 1)
        q_turned = qt_ref[at, :]
        inverse = 1.0 / (part_ref[row, :] + row_dot(norm_ref[row, :], q_turned))
        scaled = (ct_ref[at, :].astype(F32) * inverse).astype(BF16)
        inv_ref[row, :] = inverse
        scaled_ref[at, :] = scaled
        later_ref[at, :] = dot(q_turned, scaled, NT)


def near_kernel(w_ref, scaled_ref, v_ref, num_ref, gs_ref, vi_ref, plain_ref):
    for h in range(w_ref.shape[1] // HD):
        at = columns(h)
        weights, value = w_ref[:, at], v_ref[:, at]
        scaled = scaled_ref[at, :].T
        plain_ref[:, at] = scaled
        num_ref[at, :] = dot(value, weights, TN)
        gs_ref[:, at] = dot(scaled, value, NT)
        vi_ref[:, at] = dot(weights, scaled, NN)


def attend_kernel(qf_ref, qt_ref, ct_ref, inv_ref, num_ref, state_ref, ratio_ref, gden_ref, lnorm_ref):
    for h in range(inv_ref.shape[0]):
        at = columns(h)
        row = slice(h, h + 1)
        inverse = inv_ref[row, :]
        ratio = (num_ref[at, :] + dot(state_ref[at, :].astype(BF16), qt_ref[at, :], TN)) * inverse
        ratio_ref[at, :] = ratio.astype(BF16)
        grad_den = -jnp.sum(ct_ref[at, :].astype(F32) * ratio, axis=0, keepdims=True) * inverse
        gden_ref[row, :] = grad_den
        lnorm_ref[row, :] = row_dot(grad_den, qf_ref[:, at])


def query_kernel(
    q_ref, qf_ref, kf_ref, scaled_ref, ratio_ref, gden_ref, norm_ref, gs_ref, state_ref, att_ref, qg_ref, ki_ref
):
    mask = causal(q_ref.shape[0], 1)
    gden_columns = gden_ref[...].T
    for h in range(gden_ref.shape[0]):
        at = columns(h)
        grad_den = gden_columns[:, h : h + 1]
        grad_scores = jnp.where(mask, gs_ref[:, at] + grad_den, 0.0).astype(BF16)
        q_lin = dot(grad_scores, kf_ref[:, at], NN) + dot(scaled_ref[:, at], state_ref[at, :].astype(BF16), NT)
        q_lin = q_lin + grad_den * norm_ref[h : h + 1, :]
        qg_ref[:, at] = (q_lin * slope(q_ref[:, at].astype(F32))).astype(BF16)
        ki_ref[:, at] = dot(grad_scores, qf_ref[:, at], TN)
        att_ref[:, at] = ratio_ref[at, :].T


def key_kernel(k_ref, kf_ref, v_ref, ki_ref, vi_ref, lnorm_ref, later_ref, kg_ref, vg_ref):
    for h in range(k_ref.shape[1] // HD):
        at = columns(h)
        later_low = later_ref[at, :].astype(BF16)
        k_lin = ki_ref[:, at] + dot(v_ref[:, at], later_low, NT) + lnorm_ref[h : h + 1, :]
        kg_ref[:, at] = (k_lin * slope(k_ref[:, at].astype(F32))).astype(BF16)
        vg_ref[:, at] = (vi_ref[:, at] + dot(kf_ref[:, at], later_low, NN)).astype(BF16)


COST = dict(norm=1.0, state=1.0, weights=1.0, later=1.0, near=1.0, attend=1.0, query=1.0, key=1.0)
CHUNKS = ((2, 0), (2, 0))
RADIX = 2
INNER_FIRST = (True, True)
PIECE = 256
EARLY = ('S0', 'N', 'N', 'N<S0')
GATE = "S0.0.0"
NEAR_GATE = ""
QUERY_GATE = "L0.5"
LATE = ('S0', 'L0', 'S0', 'L0', 'S0', 'L0', 'S0', 'L0', 'S0', 'L0', 'S0', 'L0')
LAST = ('M', 'M', 'M', 'L0')
VMEM = 24


def call(name, kernel, outs, *args, **more):
    return pl.pallas_call(
        kernel,
        out_shape=[jax.ShapeDtypeStruct(shape, kind) for shape, kind in outs],
        compiler_params=pltpu.CompilerParams(vmem_limit_bytes=VMEM << 20),
        cost_estimate=pl.CostEstimate(flops=0, bytes_accessed=int(COST[name] * 3.5e6), transcendentals=0),
        name=name,
        **more,
    )(*args)


def bits(axis):
    return (lax.axis_size(axis) - 1).bit_length()


def swap(part, axis, mask):
    route = [(i, i ^ mask) for i in range(lax.axis_size(axis))]
    pieces = [part[at : at + PIECE] for at in range(0, part.shape[0], PIECE)]
    got = [lax.ppermute(piece, axis, route) for piece in pieces]
    return jnp.concatenate(got) if len(got) > 1 else got[0]


def is_late(axis, mask, backward):
    set_bit = (lax.axis_index(axis) >> (mask.bit_length() - 1)) & 1
    return set_bit == (0 if backward else 1)


def groups(axis, start, radix):
    spans = [(b, min(b + radix, bits(axis))) for b in range(start, bits(axis), radix)]
    return [(axis, [m << low for m in range(1, 1 << (high - low))]) for low, high in spans]


def tie(value, others):
    return lax.optimization_barrier((value, *others))[0] if others else value


def add_up(part, levels, backward):
    before = jnp.zeros_like(part)
    for axis, masks in levels:
        got = yield [(part, axis, mask) for mask in masks]
        for mask, other in zip(masks, got):
            before = before + jnp.where(is_late(axis, mask, backward), other, 0.0)
            part = part + other
    return before


def scan_small(part, backward, inner_first):
    if inner_first:
        levels = groups("inner", 0, RADIX) + [("outer", [1])] + groups("outer", 1, RADIX)
        return (yield from add_up(part, levels, backward))
    before = yield from add_up(part, [("outer", [1])] + groups("outer", 1, RADIX), backward)
    rows = part.shape[0]
    upto, result = before + part, before
    for axis, masks in groups("inner", 0, RADIX):
        both = jnp.concatenate([before, upto])
        got = yield [(both, axis, mask) for mask in masks]
        for mask, other in zip(masks, got):
            result = result + jnp.where(is_late(axis, mask, backward), other[rows:], other[:rows])
            before, upto = before + other[:rows], upto + other[rows:]
    return result


def scan_large(part, backward, chunks, joined):
    size = part.shape[0] // chunks
    parts = [part[i * size : (i + 1) * size] for i in range(chunks)]
    halving = [("inner", 1 << b) for b in range(bits("inner"))] + [("outer", 1)]
    lows = []
    for step, (axis, mask) in enumerate(halving):
        if axis == "outer":
            parts = [jnp.concatenate(parts)]
        late = is_late(axis, mask, backward)
        half = parts[0].shape[0] // 2
        sends = [jnp.where(late, part[:half], part[half:]) for part in parts]
        if step < joined:
            sends = [jnp.concatenate(sends)]
        got = yield [(send, axis, mask) for send in sends]
        if len(got) < len(parts):
            got = [got[0][i * half : (i + 1) * half] for i in range(len(parts))]
        mine = [jnp.where(late, part[half:], part[:half]) for part in parts]
        lows.append([jnp.where(late, other, own) for other, own in zip(got, mine)])
        parts = [own + other for own, other in zip(mine, got)]
    befores = [(yield from add_up(parts[0], groups("outer", 1, RADIX), backward))]
    for (axis, mask), low in zip(reversed(halving), reversed(lows)):
        if len(low) > len(befores):
            size = befores[0].shape[0] // chunks
            befores = [befores[0][i * size : (i + 1) * size] for i in range(chunks)]
        late = is_late(axis, mask, backward)
        both = [before + other for before, other in zip(befores, low)]
        got = yield [(jnp.where(late, before, full), axis, mask) for before, full in zip(befores, both)]
        mine = [jnp.where(late, full, before) for before, full in zip(befores, both)]
        befores = [
            jnp.concatenate([jnp.where(late, other, own), jnp.where(late, own, other)])
            for other, own in zip(got, mine)
        ]
    return jnp.concatenate(befores)


class Chain:
    def __init__(self, scan):
        self.scan = scan
        self.arrived = []
        self.result = None
        self.ask = next(scan)

    def hop(self, after=()):
        got = [swap(tie(part, after), axis, mask) for part, axis, mask in self.ask]
        self.arrived.append(got)
        try:
            self.ask = self.scan.send(got)
        except StopIteration as end:
            self.ask, self.result = None, end.value


def split(part, chunks, backward):
    return [Chain(scan_large(part, backward, *chunks))]


def last(chains, names):
    found = []
    for name, *place in (entry.split(".") for entry in names.split(",")):
        if name in chains and chains[name].arrived:
            arrived = chains[name].arrived
            got = arrived[min(int(place[0]), len(arrived) - 1)] if place else arrived[-1]
            found.extend(got[int(place[1]) % len(got) :][:1] if place[1:] else got)
    return found


def run(chains, order):
    for entry in order:
        name, _, others = entry.partition("<")
        if name in chains and chains[name].ask:
            chains[name].hop(last(chains, others))


def drain(chains, kind):
    ours = [chains[name] for name in sorted(chains) if name[0] == kind]
    while any(chain.ask for chain in ours):
        for chain in ours:
            if chain.ask:
                chain.hop()
    results = [chain.result for chain in ours]
    return jnp.concatenate(results) if len(results) > 1 else results[0]


def per_device(queries, keys, values, cotangent):
    tokens, width = queries.shape
    heads = width // HD
    flat, turned, square, pairs = (tokens, width), (width, tokens), (width, HD), (tokens, heads * tokens)
    small, column = (heads, HD), (heads, tokens)
    (local_norm,) = call("norm", norm_kernel, [(small, F32)], keys)
    (local_state,) = call("state", state_kernel, [(square, F32)], keys, values)
    chains = {"N": Chain(scan_small(local_norm, False, INNER_FIRST[0]))}
    chains.update(("S%d" % i, chain) for i, chain in enumerate(split(local_state, CHUNKS[0], False)))
    run(chains, EARLY)
    normal = tie(drain(chains, "N"), last(chains, GATE))
    q_feat, k_feat, q_turned, c_turned, weights, part = call(
        "weights", weights_kernel,
        [(flat, BF16), (flat, BF16), (turned, BF16), (turned, BF16), (pairs, BF16), (column, F32)],
        queries, keys, cotangent,
    )
    later_local, scaled, inverse = call(
        "later", later_kernel, [(square, F32), (turned, BF16), (column, F32)], q_turned, c_turned, part, normal
    )
    chains.update(("L%d" % i, chain) for i, chain in enumerate(split(later_local, CHUNKS[1], True)))
    run(chains, LATE)
    state = drain(chains, "S")
    near_num, near_scores, near_values, plain = call(
        "near", near_kernel, [(turned, F32), (pairs, F32), (flat, F32), (flat, BF16)], weights, tie(scaled, last(chains, NEAR_GATE)), values
    )
    ratio, grad_den, local_lnorm = call(
        "attend", attend_kernel, [(turned, BF16), (column, F32), (small, F32)],
        q_feat, q_turned, c_turned, inverse, near_num, state,
    )
    chains["M"] = Chain(scan_small(local_lnorm, True, INNER_FIRST[1]))
    run(chains, LAST)
    later_norm = drain(chains, "M")
    later = drain(chains, "L")
    attended, query_grad, near_keys = call(
        "query", query_kernel, [(flat, BF16), (flat, BF16), (flat, F32)],
        queries, q_feat, k_feat, plain, ratio, tie(grad_den, last(chains, QUERY_GATE)), normal, near_scores, state,
    )
    key_grad, value_grad = call(
        "key", key_kernel, [(flat, BF16), (flat, BF16)],
        keys, k_feat, values, near_keys, near_values, later_norm, later,
    )
    return attended, query_grad, key_grad, value_grad


def solution(mesh):
    rows = P(("outer", "inner"), None)
    return jax.shard_map(
        per_device, mesh=mesh, in_specs=(rows,) * 4, out_specs=(rows,) * 4, check_vma=False
    )
```

```python
import functools

import jax
import jax.numpy as jnp
from jax import lax
from jax.experimental import pallas as pl
from jax.experimental.pallas import tpu as pltpu
from jax.sharding import PartitionSpec as P

HD = 128
F32 = jnp.float32
BF16 = jnp.bfloat16


def features(wide):
    return jnp.where(wide > 0, wide + 1.0, jnp.exp(jnp.minimum(wide, 0.0))).astype(BF16)


def slope(wide):
    return jnp.where(wide > 0, 1.0, jnp.exp(jnp.minimum(wide, 0.0)))


def dot(a, b, contract):
    return lax.dot_general(a, b, (contract, ((), ())), preferred_element_type=F32)


NN = ((1,), (0,))
NT = ((1,), (1,))
TN = ((0,), (0,))


def columns(head):
    return slice(head * HD, (head + 1) * HD)


def causal(count, key_axis):
    keys = lax.broadcasted_iota(jnp.int32, (count, count), key_axis)
    queries = lax.broadcasted_iota(jnp.int32, (count, count), 1 - key_axis)
    return keys <= queries


def parts(row):
    high = row.astype(BF16)
    rest = row - high.astype(F32)
    middle = rest.astype(BF16)
    low = (rest - middle.astype(F32)).astype(BF16)
    return jnp.concatenate([high, middle, low], axis=0)


def row_dot(row, matrix):
    return jnp.sum(dot(parts(row), matrix, NN), axis=0, keepdims=True)


def norm_kernel(k_ref, norm_ref):
    for h in range(k_ref.shape[1] // HD):
        k_feat = features(k_ref[:, columns(h)].astype(F32))
        norm_ref[h : h + 1, :] = jnp.sum(k_feat.astype(F32), axis=0, keepdims=True)


def state_kernel(k_ref, v_ref, state_ref):
    for h in range(k_ref.shape[1] // HD):
        at = columns(h)
        state_ref[at, :] = dot(features(k_ref[:, at].astype(F32)), v_ref[:, at], TN)


def weights_kernel(q_ref, k_ref, c_ref, qf_ref, kf_ref, qt_ref, ct_ref, w_ref, part_ref):
    mask = causal(q_ref.shape[0], 0)
    for h in range(q_ref.shape[1] // HD):
        at = columns(h)
        q_feat = features(q_ref[:, at].astype(F32))
        k_feat = features(k_ref[:, at].astype(F32))
        scores = jnp.where(mask, dot(k_feat, q_feat, NT), 0.0)
        qf_ref[:, at] = q_feat
        kf_ref[:, at] = k_feat
        qt_ref[at, :] = q_feat.T
        ct_ref[at, :] = c_ref[:, at].T
        w_ref[:, at] = scores.astype(BF16)
        part_ref[h : h + 1, :] = jnp.sum(scores, axis=0, keepdims=True)


def later_kernel(qt_ref, ct_ref, part_ref, norm_ref, later_ref, scaled_ref, inv_ref):
    for h in range(part_ref.shape[0]):
        at = columns(h)
        row = slice(h, h + 1)
        q_turned = qt_ref[at, :]
        inverse = 1.0 / (part_ref[row, :] + row_dot(norm_ref[row, :], q_turned))
        scaled = (ct_ref[at, :].astype(F32) * inverse).astype(BF16)
        inv_ref[row, :] = inverse
        scaled_ref[at, :] = scaled
        later_ref[at, :] = dot(q_turned, scaled, NT)


def near_kernel(w_ref, scaled_ref, v_ref, num_ref, gs_ref, vi_ref, plain_ref):
    for h in range(w_ref.shape[1] // HD):
        at = columns(h)
        weights, value = w_ref[:, at], v_ref[:, at]
        scaled = scaled_ref[at, :].T
        plain_ref[:, at] = scaled
        num_ref[at, :] = dot(value, weights, TN)
        gs_ref[:, at] = dot(scaled, value, NT)
        vi_ref[:, at] = dot(weights, scaled, NN)


def attend_kernel(qf_ref, qt_ref, ct_ref, inv_ref, num_ref, state_ref, ratio_ref, gden_ref, lnorm_ref):
    for h in range(inv_ref.shape[0]):
        at = columns(h)
        row = slice(h, h + 1)
        inverse = inv_ref[row, :]
        ratio = (num_ref[at, :] + dot(state_ref[at, :].astype(BF16), qt_ref[at, :], TN)) * inverse
        ratio_ref[at, :] = ratio.astype(BF16)
        grad_den = -jnp.sum(ct_ref[at, :].astype(F32) * ratio, axis=0, keepdims=True) * inverse
        gden_ref[row, :] = grad_den
        lnorm_ref[row, :] = row_dot(grad_den, qf_ref[:, at])


def query_kernel(
    q_ref, qf_ref, kf_ref, scaled_ref, ratio_ref, gden_ref, norm_ref, gs_ref, state_ref, att_ref, qg_ref, ki_ref
):
    mask = causal(q_ref.shape[0], 1)
    gden_columns = gden_ref[...].T
    for h in range(gden_ref.shape[0]):
        at = columns(h)
        grad_den = gden_columns[:, h : h + 1]
        grad_scores = jnp.where(mask, gs_ref[:, at] + grad_den, 0.0).astype(BF16)
        q_lin = dot(grad_scores, kf_ref[:, at], NN) + dot(scaled_ref[:, at], state_ref[at, :].astype(BF16), NT)
        q_lin = q_lin + grad_den * norm_ref[h : h + 1, :]
        qg_ref[:, at] = (q_lin * slope(q_ref[:, at].astype(F32))).astype(BF16)
        ki_ref[:, at] = dot(grad_scores, qf_ref[:, at], TN)
        att_ref[:, at] = ratio_ref[at, :].T


def key_kernel(k_ref, kf_ref, v_ref, ki_ref, vi_ref, lnorm_ref, later_ref, kg_ref, vg_ref):
    for h in range(k_ref.shape[1] // HD):
        at = columns(h)
        later_low = later_ref[at, :].astype(BF16)
        k_lin = ki_ref[:, at] + dot(v_ref[:, at], later_low, NT) + lnorm_ref[h : h + 1, :]
        kg_ref[:, at] = (k_lin * slope(k_ref[:, at].astype(F32))).astype(BF16)
        vg_ref[:, at] = (vi_ref[:, at] + dot(kf_ref[:, at], later_low, NN)).astype(BF16)


COST = dict(norm=1.0, state=1.0, weights=1.0, later=1.0, near=1.0, attend=1.0, query=1.0, key=1.0)
CHUNKS = ((2, 0), (2, 0))
RADIX = 2
INNER_FIRST = (True, True)
PIECE = 256
EARLY = ('S0', 'N', 'N', 'N<S0')
GATE = "S0.0.0"
NEAR_GATE = ""
QUERY_GATE = "L0.5"
LATE = ('S0', 'L0', 'S0', 'L0', 'S0', 'L0', 'S0', 'L0', 'S0', 'L0', 'S0', 'L0')
LAST = ('M', 'M', 'M', 'L0')
VMEM = 24
STEPS = 2


def call(name, kernel, outs, *args, **more):
    return pl.pallas_call(
        kernel,
        out_shape=[jax.ShapeDtypeStruct(shape, kind) for shape, kind in outs],
        compiler_params=pltpu.CompilerParams(vmem_limit_bytes=VMEM << 20),
        cost_estimate=pl.CostEstimate(flops=0, bytes_accessed=int(COST[name] * 3.5e6), transcendentals=0),
        name=name,
        **more,
    )(*args)


def bits(axis):
    return (lax.axis_size(axis) - 1).bit_length()


def swap(part, axis, mask):
    route = [(i, i ^ mask) for i in range(lax.axis_size(axis))]
    pieces = [part[at : at + PIECE] for at in range(0, part.shape[0], PIECE)]
    got = [lax.ppermute(piece, axis, route) for piece in pieces]
    return jnp.concatenate(got) if len(got) > 1 else got[0]


def is_late(axis, mask, backward):
    set_bit = (lax.axis_index(axis) >> (mask.bit_length() - 1)) & 1
    return set_bit == (0 if backward else 1)


def groups(axis, start, radix):
    spans = [(b, min(b + radix, bits(axis))) for b in range(start, bits(axis), radix)]
    return [(axis, [m << low for m in range(1, 1 << (high - low))]) for low, high in spans]


def tie(value, others):
    return lax.optimization_barrier((value, *others))[0] if others else value


def add_up(part, levels, backward):
    before = jnp.zeros_like(part)
    for axis, masks in levels:
        got = yield [(part, axis, mask) for mask in masks]
        for mask, other in zip(masks, got):
            before = before + jnp.where(is_late(axis, mask, backward), other, 0.0)
            part = part + other
    return before


def scan_small(part, backward, inner_first):
    if inner_first:
        levels = groups("inner", 0, RADIX) + [("outer", [1])] + groups("outer", 1, RADIX)
        return (yield from add_up(part, levels, backward))
    before = yield from add_up(part, [("outer", [1])] + groups("outer", 1, RADIX), backward)
    rows = part.shape[0]
    upto, result = before + part, before
    for axis, masks in groups("inner", 0, RADIX):
        both = jnp.concatenate([before, upto])
        got = yield [(both, axis, mask) for mask in masks]
        for mask, other in zip(masks, got):
            result = result + jnp.where(is_late(axis, mask, backward), other[rows:], other[:rows])
            before, upto = before + other[:rows], upto + other[rows:]
    return result


def scan_large(part, backward, chunks, joined):
    size = part.shape[0] // chunks
    parts = [part[i * size : (i + 1) * size] for i in range(chunks)]
    halving = [("inner", 1 << b) for b in range(bits("inner"))] + [("outer", 1)]
    lows = []
    for step, (axis, mask) in enumerate(halving):
        if axis == "outer":
            parts = [jnp.concatenate(parts)]
        late = is_late(axis, mask, backward)
        half = parts[0].shape[0] // 2
        sends = [jnp.where(late, part[:half], part[half:]) for part in parts]
        if step < joined:
            sends = [jnp.concatenate(sends)]
        got = yield [(send, axis, mask) for send in sends]
        if len(got) < len(parts):
            got = [got[0][i * half : (i + 1) * half] for i in range(len(parts))]
        mine = [jnp.where(late, part[half:], part[:half]) for part in parts]
        lows.append([jnp.where(late, other, own) for other, own in zip(got, mine)])
        parts = [own + other for own, other in zip(mine, got)]
    befores = [(yield from add_up(parts[0], groups("outer", 1, RADIX), backward))]
    for (axis, mask), low in zip(reversed(halving), reversed(lows)):
        if len(low) > len(befores):
            size = befores[0].shape[0] // chunks
            befores = [befores[0][i * size : (i + 1) * size] for i in range(chunks)]
        late = is_late(axis, mask, backward)
        both = [before + other for before, other in zip(befores, low)]
        got = yield [(jnp.where(late, before, full), axis, mask) for before, full in zip(befores, both)]
        mine = [jnp.where(late, full, before) for before, full in zip(befores, both)]
        befores = [
            jnp.concatenate([jnp.where(late, other, own), jnp.where(late, own, other)])
            for other, own in zip(got, mine)
        ]
    return jnp.concatenate(befores)


class Chain:
    def __init__(self, scan):
        self.scan = scan
        self.arrived = []
        self.result = None
        self.ask = next(scan)

    def hop(self, after=()):
        got = [swap(tie(part, after), axis, mask) for part, axis, mask in self.ask]
        self.arrived.append(got)
        try:
            self.ask = self.scan.send(got)
        except StopIteration as end:
            self.ask, self.result = None, end.value


def split(part, chunks, backward):
    return [Chain(scan_large(part, backward, *chunks))]


def last(chains, names):
    found = []
    for name, *place in (entry.split(".") for entry in names.split(",")):
        if name in chains and chains[name].arrived:
            arrived = chains[name].arrived
            got = arrived[min(int(place[0]), len(arrived) - 1)] if place else arrived[-1]
            found.extend(got[int(place[1]) % len(got) :][:1] if place[1:] else got)
    return found


def run(chains, order):
    for entry in order:
        name, _, others = entry.partition("<")
        if name in chains and chains[name].ask:
            chains[name].hop(last(chains, others))


def drain(chains, kind):
    ours = [chains[name] for name in sorted(chains) if name[0] == kind]
    while any(chain.ask for chain in ours):
        for chain in ours:
            if chain.ask:
                chain.hop()
    results = [chain.result for chain in ours]
    return jnp.concatenate(results) if len(results) > 1 else results[0]


def per_device(queries, keys, values, cotangent):
    tokens, width = queries.shape
    heads = width // HD
    flat, turned, square, pairs = (tokens, width), (width, tokens), (width, HD), (tokens, heads * tokens)
    small, column = (heads, HD), (heads, tokens)
    (local_norm,) = call("norm", norm_kernel, [(small, F32)], keys)
    (local_state,) = call("state", state_kernel, [(square, F32)], keys, values)
    chains = {"N": Chain(scan_small(local_norm, False, INNER_FIRST[0]))}
    chains.update(("S%d" % i, chain) for i, chain in enumerate(split(local_state, CHUNKS[0], False)))
    run(chains, EARLY)
    normal = tie(drain(chains, "N"), last(chains, GATE))
    q_feat, k_feat, q_turned, c_turned, weights, part = call(
        "weights", weights_kernel,
        [(flat, BF16), (flat, BF16), (turned, BF16), (turned, BF16), (pairs, BF16), (column, F32)],
        queries, keys, cotangent,
    )
    later_local, scaled, inverse = call(
        "later", later_kernel, [(square, F32), (turned, BF16), (column, F32)], q_turned, c_turned, part, normal
    )
    chains.update(("L%d" % i, chain) for i, chain in enumerate(split(later_local, CHUNKS[1], True)))
    run(chains, LATE)
    state = drain(chains, "S")
    near_num, near_scores, near_values, plain = call(
        "near", near_kernel, [(turned, F32), (pairs, F32), (flat, F32), (flat, BF16)], weights, tie(scaled, last(chains, NEAR_GATE)), values
    )
    ratio, grad_den, local_lnorm = call(
        "attend", attend_kernel, [(turned, BF16), (column, F32), (small, F32)],
        q_feat, q_turned, c_turned, inverse, near_num, state,
    )
    chains["M"] = Chain(scan_small(local_lnorm, True, INNER_FIRST[1]))
    run(chains, LAST)
    later_norm = drain(chains, "M")
    later = drain(chains, "L")
    attended, query_grad, near_keys = call(
        "query", query_kernel, [(flat, BF16), (flat, BF16), (flat, F32)],
        queries, q_feat, k_feat, plain, ratio, tie(grad_den, last(chains, QUERY_GATE)), normal, near_scores, state,
    )
    across = pl.BlockSpec((tokens, width // STEPS), lambda step: (0, step))
    down = lambda step: (step, 0)
    key_grad, value_grad = call(
        "key", key_kernel, [(flat, BF16), (flat, BF16)],
        keys, k_feat, values, near_keys, near_values, later_norm, later,
        grid=(STEPS,),
        in_specs=[across] * 5 + [pl.BlockSpec((heads // STEPS, HD), down), pl.BlockSpec((width // STEPS, HD), down)],
        out_specs=[across] * 2,
    )
    return attended, query_grad, key_grad, value_grad


def solution(mesh):
    rows = P(("outer", "inner"), None)
    return jax.shard_map(
        per_device, mesh=mesh, in_specs=(rows,) * 4, out_specs=(rows,) * 4, check_vma=False
    )
```
